128 devices in a mesh: sample: 16 (over z_hi, x, core), tensor: 8 (over z_lo, y).
Axes of the slice: x: 4, y: 4, z: 4 (z_hi: 2, z_lo: 2; z = z_hi * 2 + z_lo), core: 2. Of those that a mesh axis runs over, the one named last changes fastest.
Arguments:
- stepwise_feed_vectors: bfloat16 [4, 64, 8192], P(None, 'sample'), may hold values from -6 to 6
- prelude_rescaling_factor: bfloat16 [8192], replicated, may hold values from 0.099609375 to 1.8984375
- probe_mapping_matrix: bfloat16 [8192, 8, 1024], P('sample', 'tensor'), may hold values from -0.125 to 0.125
- paired_mapping_matrix: bfloat16 [8192, 8, 256], P('sample', 'tensor'), may hold values from -0.0625 to 0.0625
- final_mapping_matrix: bfloat16 [8192, 8, 1024], P('sample', 'tensor'), may hold values from -0.1875 to 0.1875
- memory_pair_tensor: bfloat16 [256, 8, 2, 512, 128], P('sample', 'tensor'), may hold values from -240 to 240, as said below
- retained_draw_ids: int32 [64], replicated, may hold values from 0 to 255, as said below
- valid_extents: int32 [256], replicated, may hold values from 64 to 512, as said below
Outputs:
- attn_out: bfloat16 [4, 64, 8192], P(None, 'sample', 'tensor')
The draws below stay inside these ranges and needn't reach their ends.
Inputs may be any that keep to these rules, and one draw needn't show every extreme that they name: `retained_draw_ids`: 64 distinct sampled rows; surviving rows g * 16 to (g + 1) * 16 - 1 form group g. Within one group at most 2 survivors lie in one aligned block of 16 sampled rows, and in every group some block holds exactly 2. `valid_extents`: some sampled rows of every draw use all 512 positions, among them a survivor of each group. `memory_pair_tensor`: keys and values of the sampled rows' caches.
All inputs are finite; a program needn't handle non-finite values.
Results may differ from the reference program's by a relative error of at most 0.02.
The reference program's roundings to bfloat16 on the way count: a program that leaves them out, or rounds other values in their place, can miss the bound.
Values may be sent and summed in bfloat16 or wider, within the bound.
No kernel may reach another device: no remote copies, remote signals or barrier semaphores. Data moves between devices by JAX's collectives and lax.ppermute only.
A program may use at most 128 MiB of HBM per device.

```python
import jax
import jax.numpy as jnp
from jax import lax

D = 8192
PER_HEAD_SPAN = 128
GQA = 8
ROWS_DEV = 16
SURV_GRP = 16
CAP = 2
STEPS = 4
MEMORY_SLOTS = 512
PAIRED_GROUPS = 8
ROWS = 256
LIVE_STREAMS = 64


def permute_rows(row_key):
    return jax.random.permutation(row_key, ROWS_DEV)


def remaining_sample_rows(key):
    key = jax.random.fold_in(key, 11)
    blocks = ROWS // ROWS_DEV
    group_count = LIVE_STREAMS // SURV_GRP
    pieces = []
    for group_number in range(group_count):
        group_key = jax.random.fold_in(key, group_number)
        forced_key, order_key, shuffle_key = jax.random.split(group_key, 3)
        forced = jax.random.randint(forced_key, (1,), 0, blocks)
        slot_order = jax.random.permutation(order_key, CAP * (blocks - 1))[:SURV_GRP - CAP]
        others = slot_order // CAP
        others = others + (others >= forced[0]).astype(jnp.int32)
        selected_rows = jnp.concatenate([jnp.broadcast_to(forced, (CAP,)), others])
        shuffle = jax.random.permutation(shuffle_key, SURV_GRP)
        pieces.append(selected_rows[shuffle])
    parent_strands = jnp.concatenate(pieces).astype(jnp.int32)
    position = jnp.arange(parent_strands.shape[0])
    earlier = jnp.sum((parent_strands[:, None] == parent_strands[None, :]) & (position[None, :] < position[:, None]), axis=1).astype(jnp.int32)
    row_orders = jax.vmap(permute_rows)(jax.random.split(jax.random.fold_in(key, 999), blocks))
    local_rows = row_orders[parent_strands, earlier]
    return (parent_strands * ROWS_DEV + local_rows).astype(jnp.int32)


def draw_retained_draw_ids(key, part):
    return remaining_sample_rows(key)


def draw_valid_extents(key, part):
    selected_rows = remaining_sample_rows(key)
    key = jax.random.fold_in(key, 5)
    base_key, full_key = jax.random.split(key)
    normal_part = jax.random.randint(base_key, (ROWS,), MEMORY_SLOTS // 8, MEMORY_SLOTS + 1)
    full_rows = jax.random.randint(full_key, (ROWS,), 0, 4) == 0
    result = jnp.where(full_rows, MEMORY_SLOTS, normal_part)
    result = result.at[selected_rows[::SURV_GRP]].set(MEMORY_SLOTS)
    return result.astype(jnp.int32)


def draw_memory_pair_tensor(key, part):
    key = jax.random.fold_in(key, 7)
    base_key = jax.random.fold_in(key, 0)
    array_shape = (ROWS, PAIRED_GROUPS, 2, MEMORY_SLOTS, PER_HEAD_SPAN)
    normal_part = jax.random.normal(base_key, array_shape, jnp.float32)
    result = normal_part
    return result.astype(jnp.bfloat16)


def level_of(stream_key, shape, shards, low, largest):
    def one(axis_at, shards_of):
        steps = jax.random.uniform(jax.random.fold_in(jax.random.fold_in(stream_key, 6), axis_at), (shards_of,), jnp.float32, low / len(shards), largest / len(shards))
        return jnp.repeat(jnp.exp(steps), shape[axis_at] // shards_of).reshape((-1,) + (1,) * (len(shape) - axis_at - 1))

    level = one(*shards[0])
    for cut in shards[1:]:
        level = level * one(*cut)
    return level


def gaussian(stream_key, shape, scale, reach, cuts=(), kind=jnp.bfloat16):
    factor_of = level_of(stream_key, shape, cuts, -0.22, 0.18) if cuts else 1.0
    values = jax.random.normal(stream_key, shape, jnp.float32) * scale * factor_of
    return jnp.minimum(jnp.maximum(values, -reach), reach).astype(kind)


def setup_inputs(seed: int = 0) -> dict:
    splits = jax.random.split(jax.random.key(seed), 9)
    stepwise_feed_vectors = gaussian(splits[0], (STEPS, LIVE_STREAMS, D), 1.0, 6.0, ((1, 16),))
    prelude_rescaling_factor = jnp.clip(1.0 + 0.18 * jax.random.normal(splits[1], (D,), jnp.float32), 0.099609375, 1.8984375).astype(jnp.bfloat16)
    probe_mapping_matrix = gaussian(splits[2], (D, PAIRED_GROUPS, GQA * PER_HEAD_SPAN), (D // 4) ** -0.5, 0.125, ((0, 16), (1, 8)))
    paired_mapping_matrix = gaussian(splits[3], (D, PAIRED_GROUPS, 2 * PER_HEAD_SPAN), D ** -0.5, 0.0625, ((0, 16), (1, 8)))
    final_mapping_matrix = gaussian(splits[4], (D, PAIRED_GROUPS, GQA * PER_HEAD_SPAN), (GQA * PER_HEAD_SPAN) ** -0.5, 0.1875, ((0, 16), (1, 8)))
    memory_pair_tensor = draw_memory_pair_tensor(jax.random.fold_in(splits[8], 71), 0)
    retained_draw_ids = draw_retained_draw_ids(jax.random.fold_in(splits[8], 71), 0)
    valid_extents = draw_valid_extents(jax.random.fold_in(splits[8], 71), 0)
    return {"stepwise_feed_vectors": stepwise_feed_vectors, "prelude_rescaling_factor": prelude_rescaling_factor, "probe_mapping_matrix": probe_mapping_matrix, "paired_mapping_matrix": paired_mapping_matrix, "final_mapping_matrix": final_mapping_matrix, "memory_pair_tensor": memory_pair_tensor, "retained_draw_ids": retained_draw_ids, "valid_extents": valid_extents}


norm_eps = 1e-05

def attend(query_vectors, memory_element_tally, latest_projection, valid_extent_bounds):
    key_rows = memory_element_tally[:, 0].astype(jnp.float32)
    cached_value_rows = memory_element_tally[:, 1].astype(jnp.float32)
    softmax_scale = query_vectors.shape[-1] ** (-0.5)
    expanded_query_rows = query_vectors.astype(jnp.float32)
    cached_scores = jnp.einsum('bsgd,bcd->bsgc', expanded_query_rows, key_rows) * softmax_scale
    extent = key_rows.shape[1]
    cached_scores = jnp.where(jnp.arange(extent)[None, None, None, :] < valid_extent_bounds[:, None, None, None], cached_scores, -jnp.inf)
    latest_key_rows = latest_projection[:, :, 0].astype(jnp.float32)
    latest_value_rows = latest_projection[:, :, 1].astype(jnp.float32)
    latest_token_scores = jnp.einsum('rauv,rnv->raun', expanded_query_rows, latest_key_rows) * softmax_scale
    step_count = latest_projection.shape[1]
    causal = jnp.arange(step_count)[None, :] <= jnp.arange(step_count)[:, None]
    latest_token_scores = jnp.where(causal[None, :, None, :], latest_token_scores, -jnp.inf)
    highest = jnp.maximum(lax.optimization_barrier(jnp.max(cached_scores, -1)), lax.optimization_barrier(jnp.max(latest_token_scores, -1)))
    cached_probs = jnp.exp(cached_scores - highest[..., None])
    fresh_probs = jnp.exp(latest_token_scores - highest[..., None])
    totals = lax.optimization_barrier(jnp.sum(cached_probs, -1)) + lax.optimization_barrier(jnp.sum(fresh_probs, -1))
    stored_position_weights = cached_probs.astype(jnp.bfloat16).astype(jnp.float32)
    latest_token_weights = fresh_probs.astype(jnp.bfloat16).astype(jnp.float32)
    weighted_value_sum = jnp.einsum('mijl,mlt->mijt', stored_position_weights, cached_value_rows) + jnp.einsum('hiax,hxm->hiam', latest_token_weights, latest_value_rows)
    result = (weighted_value_sum / totals[..., None]).astype(jnp.bfloat16)
    return result.reshape(result.shape[0], result.shape[1], result.shape[2] * result.shape[3])

def reference(stepwise_feed_vectors, prelude_rescaling_factor, probe_mapping_matrix, paired_mapping_matrix, final_mapping_matrix, memory_pair_tensor, retained_draw_ids, valid_extents):
    widened = stepwise_feed_vectors.astype(jnp.float32)
    normed = (widened * lax.rsqrt(lax.optimization_barrier(jnp.mean(widened * widened, -1, keepdims=True)) + norm_eps) * prelude_rescaling_factor.astype(jnp.float32)).astype(jnp.bfloat16)
    flat_rows = normed.reshape(STEPS * LIVE_STREAMS, D)
    query_vectors = jnp.dot(flat_rows, probe_mapping_matrix.reshape(D, PAIRED_GROUPS * GQA * PER_HEAD_SPAN), preferred_element_type=jnp.float32).astype(jnp.bfloat16)
    latest_projection = jnp.dot(flat_rows, paired_mapping_matrix.reshape(D, PAIRED_GROUPS * 2 * PER_HEAD_SPAN), preferred_element_type=jnp.float32).astype(jnp.bfloat16)
    query_vectors = query_vectors.reshape(STEPS, LIVE_STREAMS, PAIRED_GROUPS, GQA, PER_HEAD_SPAN).transpose(1, 2, 0, 3, 4).reshape(LIVE_STREAMS * PAIRED_GROUPS, STEPS, GQA, PER_HEAD_SPAN)
    latest_projection = latest_projection.reshape(STEPS, LIVE_STREAMS, PAIRED_GROUPS, 2, PER_HEAD_SPAN).transpose(1, 2, 0, 3, 4).reshape(LIVE_STREAMS * PAIRED_GROUPS, STEPS, 2, PER_HEAD_SPAN)
    memory_element_tally = jnp.take(memory_pair_tensor, retained_draw_ids, axis=0).reshape(LIVE_STREAMS * PAIRED_GROUPS, 2, MEMORY_SLOTS, PER_HEAD_SPAN)
    valid_extent_bounds = jnp.repeat(jnp.take(valid_extents, retained_draw_ids), PAIRED_GROUPS)
    attended = attend(query_vectors, memory_element_tally, latest_projection, valid_extent_bounds)
    attended = attended.reshape(LIVE_STREAMS, PAIRED_GROUPS, STEPS, GQA * PER_HEAD_SPAN).transpose(2, 0, 1, 3).reshape(STEPS * LIVE_STREAMS, PAIRED_GROUPS * GQA * PER_HEAD_SPAN)
    mixed = jnp.dot(attended, final_mapping_matrix.reshape(D, PAIRED_GROUPS * GQA * PER_HEAD_SPAN).T, preferred_element_type=jnp.float32)
    return mixed.reshape(STEPS, LIVE_STREAMS, D).astype(jnp.bfloat16)
```

```python
import functools

import jax
import jax.numpy as jnp
from jax import lax
from jax.experimental import pallas as pl
from jax.experimental.pallas import tpu as pltpu
from jax.sharding import PartitionSpec as P

NORM_EPS = 1e-05
SLOTS = 8
VMEM = pl.BlockSpec(memory_space=pltpu.VMEM)
SMEM = pl.BlockSpec(memory_space=pltpu.SMEM)
ANY = pl.BlockSpec(memory_space=pl.ANY)
F32 = jnp.float32
BF16 = jnp.bfloat16


def normalize_kernel(x_ref, gain_ref, out_ref, rows):
    steps, held, width = x_ref.shape
    blocks, _, block = out_ref.shape
    gain = gain_ref[...].astype(F32)
    for i in range(steps):
        x = x_ref[i].astype(F32)
        scale = lax.rsqrt(jnp.mean(x * x, -1, keepdims=True) + NORM_EPS)
        rows[held * i : held * (i + 1), :] = x * scale * gain
    for b in range(blocks):
        out_ref[b] = rows[:, block * b : block * (b + 1)].astype(BF16)


def project_kernel(place_ref, x_ref, q_ref, kv_ref, out_ref):
    padded, rows = out_ref.shape[0], x_ref.shape[0]
    spread = (
        lax.broadcasted_iota(jnp.int32, (padded, rows), 0) == place_ref[...]
    ).astype(BF16)
    x = jnp.dot(spread, x_ref[...], preferred_element_type=F32).astype(BF16)
    width = q_ref.shape[1]
    for c in range(0, width, 256):
        out_ref[:, c : c + 256] = jnp.dot(
            x, q_ref[:, c : c + 256], preferred_element_type=F32
        ).astype(BF16)
    out_ref[:, width:] = jnp.dot(x, kv_ref[...], preferred_element_type=F32).astype(BF16)


def attend_kernel(heads, steps, ids_ref, extents_ref, part_ref, cache_ref, out_ref, cache, summed, answer, picked, sems):
    me = lax.axis_index("sample")
    owned = cache_ref.shape[0]
    head = cache_ref.shape[-1]
    extent = cache_ref.shape[-2]
    rows = steps * SLOTS
    for k in range(SLOTS):
        picked[k] = 0

    def look(j, found):
        row = ids_ref[j]
        mine = row // owned == me

        @pl.when(mine)
        def _():
            picked[found] = row % owned

        return found + mine.astype(jnp.int32)

    lax.fori_loop(0, ids_ref.shape[0], look, 0)
    copies = [
        pltpu.make_async_copy(cache_ref.at[picked[k]], cache.at[k], sems.at[k]) for k in range(SLOTS)
    ]
    for copy in copies:
        copy.start()
    for c in range(heads + 2):
        total = part_ref[0, :, head * c : head * (c + 1)].astype(F32)
        for source in range(1, part_ref.shape[0]):
            total = total + part_ref[source, :, head * c : head * (c + 1)].astype(F32)
        summed[rows * c : rows * (c + 1), :] = total
    many = heads * steps
    step_of = lax.broadcasted_iota(jnp.int32, (many, 16), 0) % steps
    fresh_at = lax.broadcasted_iota(jnp.int32, (many, 16), 1)
    causal = fresh_at <= step_of
    position = lax.broadcasted_iota(jnp.int32, (many, extent), 1)
    scale = head**-0.5
    nothing = jnp.zeros((16 - steps, head), F32)
    last = (((1,), (1,)), ((), ()))
    for k in range(SLOTS):
        query = summed[pl.ds(k, many, stride=SLOTS), :].astype(BF16)
        fresh_key = jnp.concatenate(
            [summed[pl.ds(rows * heads + k, steps, stride=SLOTS), :], nothing], 0
        ).astype(BF16)
        fresh_value = jnp.concatenate(
            [summed[pl.ds(rows * (heads + 1) + k, steps, stride=SLOTS), :], nothing], 0
        ).astype(BF16)
        length = extents_ref[me * owned + picked[k]]
        copies[k].wait()
        score = lax.dot_general(query, cache[k, 0], last, preferred_element_type=F32) * scale
        score = jnp.where(position < length, score, -jnp.inf)
        fresh = lax.dot_general(query, fresh_key, last, preferred_element_type=F32) * scale
        fresh = jnp.where(causal, fresh, -jnp.inf)
        highest = jnp.maximum(
            jnp.max(score, -1, keepdims=True), jnp.max(fresh, -1, keepdims=True)
        )
        probs = jnp.exp(score - highest)
        fresh_probs = jnp.exp(fresh - highest)
        total = jnp.sum(probs, -1, keepdims=True) + jnp.sum(fresh_probs, -1, keepdims=True)
        value = jnp.dot(probs.astype(BF16), cache[k, 1], preferred_element_type=F32)
        value = value + jnp.dot(fresh_probs.astype(BF16), fresh_value, preferred_element_type=F32)
        answer[pl.ds(k, many, stride=SLOTS), :] = value / total
    for h in range(heads):
        out_ref[:, head * h : head * (h + 1)] = answer[rows * h : rows * (h + 1), :].astype(BF16)


def output_kernel(place_ref, att_ref, w_ref, out_ref):
    rows, padded = out_ref.shape[0], att_ref.shape[0]
    pick = (lax.broadcasted_iota(jnp.int32, (rows, padded), 1) == place_ref[...]).astype(BF16)
    att = jnp.dot(pick, att_ref[...], preferred_element_type=F32).astype(BF16)
    for c in range(0, out_ref.shape[1], 256):
        out_ref[:, c : c + 256] = lax.dot_general(
            att, w_ref[c : c + 256, :], (((1,), (1,)), ((), ())), preferred_element_type=F32
        ).astype(BF16)


def coordinates(device):
    s, t = divmod(device, 8)
    return s >> 3, (s >> 1) & 3, s & 1, t >> 2, t & 3


def index_of(z_hi, x, core, z_lo, y):
    return ((z_hi * 4 + x) * 2 + core) * 8 + z_lo * 4 + y


def send(value, where):
    return lax.ppermute(
        value, ("sample", "tensor"), [(d, index_of(*where(*coordinates(d)))) for d in range(128)]
    )


def per_device(x, gain, probe, paired, final, memory, ids, extents):
    blocks = lax.axis_size("sample")
    parts = lax.axis_size("tensor")
    steps, held, width = x.shape
    block = width // blocks
    survivors = ids.shape[0]
    owned, _, _, extent, head = memory.shape
    q_width = probe.shape[2]
    heads = q_width // head
    kv_width = paired.shape[2]
    rows = steps * survivors
    slot_rows = steps * SLOTS
    padded = blocks * slot_rows

    owner = ids // owned
    at = jnp.arange(survivors)
    slot = jnp.sum((owner[:, None] == owner[None, :]) & (at[None, :] < at[:, None]), 1)
    place = (owner * slot_rows + slot).astype(jnp.int32)
    step_at = jnp.arange(steps, dtype=jnp.int32) * SLOTS
    place_in = (place.reshape(blocks, 1, held) + step_at[None, :, None]).reshape(1, rows)
    place_out = (place.reshape(blocks, 1, held) + step_at[None, :, None]).reshape(rows, 1)

    normed = pl.pallas_call(
        normalize_kernel,
        out_shape=jax.ShapeDtypeStruct((blocks, steps * held, block), BF16),
        in_specs=[VMEM, VMEM],
        out_specs=VMEM,
        scratch_shapes=[pltpu.VMEM((steps * held, width), F32)],
        name="normalize",
    )(x, gain.reshape(1, width))
    arrived = lax.all_to_all(normed, "sample", split_axis=0, concat_axis=0, tiled=True)

    partial = pl.pallas_call(
        project_kernel,
        out_shape=jax.ShapeDtypeStruct((padded, q_width + kv_width), BF16),
        in_specs=[VMEM] * 4,
        out_specs=VMEM,
        name="project",
        compiler_params=pltpu.CompilerParams(vmem_limit_bytes=24 << 20),
    )(place_in, arrived.reshape(rows, block), probe.reshape(block, q_width), paired.reshape(block, kv_width))
    mine = lax.all_to_all(
        partial.reshape(blocks, slot_rows, q_width + kv_width), "sample", split_axis=0, concat_axis=0, tiled=True
    )

    attended = pl.pallas_call(
        functools.partial(attend_kernel, heads, steps),
        out_shape=jax.ShapeDtypeStruct((slot_rows, q_width), BF16),
        in_specs=[SMEM, SMEM, VMEM, ANY],
        out_specs=VMEM,
        scratch_shapes=[
            pltpu.VMEM((SLOTS, 2, extent, head), BF16),
            pltpu.VMEM((slot_rows * (heads + 2), head), F32),
            pltpu.VMEM((slot_rows * heads, head), F32),
            pltpu.SMEM((SLOTS,), jnp.int32),
            pltpu.SemaphoreType.DMA((SLOTS,)),
        ],
        name="attend",
        compiler_params=pltpu.CompilerParams(vmem_limit_bytes=24 << 20),
    )(ids, extents, mine, memory.reshape(owned, 2, extent, head))
    gathered = lax.all_to_all(
        jnp.broadcast_to(attended[None], (blocks,) + attended.shape), "sample", split_axis=0, concat_axis=0, tiled=True
    )

    out = pl.pallas_call(
        output_kernel,
        out_shape=jax.ShapeDtypeStruct((rows, block), BF16),
        in_specs=[VMEM] * 3,
        out_specs=VMEM,
        name="output",
        compiler_params=pltpu.CompilerParams(vmem_limit_bytes=24 << 20),
    )(place_out, gathered.reshape(padded, q_width), final.reshape(block, q_width))
    out = lax.all_to_all(
        out.reshape(parts, rows // parts, block), "tensor", split_axis=0, concat_axis=0, tiled=True
    )
    out = jnp.sum(out.astype(F32), 0).astype(BF16).reshape(2, steps * held, block)
    core = lax.axis_index("sample") % 2
    kept = lax.dynamic_index_in_dim(out, core, 0, keepdims=False)
    other = send(
        lax.dynamic_index_in_dim(out, 1 - core, 0, keepdims=False),
        lambda z_hi, x, core, z_lo, y: (z_hi, x, 1 - core, z_lo, y),
    )
    both = jnp.where(core == 0, jnp.concatenate([kept, other], 1), jnp.concatenate([other, kept], 1))
    return send(both, lambda z_hi, x, core, z_lo, y: (z_lo, y, core, z_hi, x)).reshape(
        steps, held, width // parts
    )


def solution(mesh):
    placed = (
        P(None, "sample", None),
        P(),
        P("sample", "tensor", None),
        P("sample", "tensor", None),
        P("sample", "tensor", None),
        P("sample", "tensor", None, None, None),
        P(),
        P(),
    )
    return jax.shard_map(
        per_device,
        mesh=mesh,
        in_specs=placed,
        out_specs=P(None, "sample", "tensor"),
        check_vma=False,
    )
```

```python
import functools

import jax
import jax.numpy as jnp
import numpy as np
from jax import lax
from jax.experimental import pallas as pl
from jax.experimental.pallas import tpu as pltpu
from jax.sharding import PartitionSpec as P

NORM_EPS = 1e-05
ROWS_ORDER = np.array([4, 5, 3, 7, 0, 1, 2, 6])
QUERY_ORDER = np.array([7, 6, 5, 4, 3, 2, 1, 0])
ATTENDED_ORDER = np.array([4, 5, 6, 2, 0, 1, 7, 3])
OUT_ORDER = np.array([2, 6, 5, 4, 3, 7, 1, 0])
SLOTS = 8
VMEM = pl.BlockSpec(memory_space=pltpu.VMEM)
SMEM = pl.BlockSpec(memory_space=pltpu.SMEM)
ANY = pl.BlockSpec(memory_space=pl.ANY)
F32 = jnp.float32
BF16 = jnp.bfloat16
I32 = jnp.int32
LAST = (((1,), (1,)), ((), ()))
FIRST = (((0,), (0,)), ((), ()))


def place_of(s, t):
    return s >> 3, (s >> 1) & 3, s & 1, t >> 2, t & 3


def send(value, where):
    pairs = []
    for device in range(128):
        z_hi, x, core, z_lo, y = where(*place_of(*divmod(device, 8)))
        pairs.append((device, ((z_hi * 4 + x) * 2 + core) * 8 + z_lo * 4 + y))
    return lax.ppermute(value, ("sample", "tensor"), pairs)


def to_core(z_hi, x, core, z_lo, y):
    return z_hi, x, 1 - core, z_lo, y


def summed_at(x, y):
    return (2 * x + 2 - y) & 3


def to_rows(z_hi, x, core, z_lo, y):
    return z_lo, summed_at(x, y), core, z_hi, x


def exchange_chips(value, order):
    return lax.all_to_all(
        value,
        "sample",
        split_axis=0,
        concat_axis=0,
        tiled=True,
        axis_index_groups=[[2 * chip + core for chip in order.tolist()] for core in range(2)],
    )


def exchange_rows(value):
    groups = [
        [(chip * 2 + core) * 8 + (z_lo ^ (chip >> 2)) * 4 + y for chip in ROWS_ORDER.tolist()]
        for core in range(2)
        for z_lo in range(2)
        for y in range(4)
    ]
    return lax.all_to_all(
        value, ("sample", "tensor"), split_axis=0, concat_axis=0, tiled=True, axis_index_groups=groups
    )


def exchange_heads(value):
    return lax.all_to_all(
        value, "tensor", split_axis=0, concat_axis=0, tiled=True, axis_index_groups=[OUT_ORDER.tolist()]
    )


def entry(order, at):
    found = 0
    for n, value in enumerate(order.tolist()):
        found = jnp.where(at == n, value, found)
    return found


def normalize_kernel(x_ref, gain_ref, out_ref, x_here, gain_here, rows, sems):
    steps, held, width = x_ref.shape
    chips, _, block = out_ref.shape
    gain_copy = pltpu.make_async_copy(gain_ref, gain_here, sems.at[0])
    x_copy = pltpu.make_async_copy(x_ref, x_here, sems.at[1])
    gain_copy.start()
    x_copy.start()
    gain_copy.wait()
    gain = gain_here[...].astype(F32).reshape(1, width)
    x_copy.wait()
    for i in range(steps):
        x = x_here[i].astype(F32)
        scale = lax.rsqrt(jnp.mean(x * x, -1, keepdims=True) + NORM_EPS)
        rows[held * i : held * (i + 1), :] = x * scale * gain
    for m in range(chips):
        at = block * int(ROWS_ORDER[m])
        out_ref[m] = rows[:, at : at + block].astype(BF16)


def project_kernel(key_ref, near_ref, far_ref, q_ref, kv_ref, out_ref, chosen):
    chips, rows, _ = out_ref.shape
    padded = chips * rows
    half = near_ref.shape[0]
    spread = (
        lax.broadcasted_iota(I32, (padded, 2 * half), 0) == key_ref[...]
    ).astype(BF16)
    x = jnp.dot(spread[:, :half], near_ref[...], preferred_element_type=F32)
    x = x + jnp.dot(spread[:, half:], far_ref[...], preferred_element_type=F32)
    chosen[...] = x.astype(BF16)
    core = lax.axis_index("sample") % 2
    block, width = q_ref.shape[0] // 2, q_ref.shape[1]
    mine = chosen[:, pl.ds(pl.multiple_of(core * block, block), block)]
    other = chosen[:, pl.ds(pl.multiple_of((1 - core) * block, block), block)]
    for c in range(0, width + kv_ref.shape[1], 256):
        w_ref, at = (q_ref, c) if c < width else (kv_ref, 0)
        w, w2 = w_ref[:block, at : at + 256], w_ref[block:, at : at + 256]
        part = jnp.dot(mine, w, preferred_element_type=F32)
        part = part + jnp.dot(other, w2, preferred_element_type=F32)
        part = part.astype(BF16)
        for m in range(chips):
            out_ref[m, :, c : c + 256] = part[rows * m : rows * (m + 1)]


def attend_kernel(heads, steps, picked_ref, length_ref, part_ref, cache_ref, out_ref, summed, answer):
    head = cache_ref.shape[-1]
    extent = cache_ref.shape[-2]
    rows = steps * SLOTS
    for c in range(heads + 2):
        total = part_ref[0, :, head * c : head * (c + 1)].astype(F32)
        for source in range(1, part_ref.shape[0]):
            total = total + part_ref[source, :, head * c : head * (c + 1)].astype(F32)
        summed[rows * c : rows * (c + 1), :] = total
    many = heads * steps
    scale = head**-0.5
    position = lax.broadcasted_iota(I32, (many, extent), 1)
    fresh_at = lax.broadcasted_iota(I32, (many, head), 1)
    causal = fresh_at <= lax.broadcasted_iota(I32, (many, head), 0) % steps
    nothing = jnp.zeros((head - steps, head), F32)

    def fresh(k, which):
        rows_at = pl.ds(rows * (heads + which) + k, steps, stride=SLOTS)
        return jnp.concatenate([summed[rows_at, :], nothing], 0).astype(BF16)

    scores = []
    for k in range(SLOTS):
        query = summed[pl.ds(k, many, stride=SLOTS), :].astype(BF16)
        scores.append(
            (
                lax.dot_general(query, cache_ref[picked_ref[k], 0], LAST, preferred_element_type=F32),
                lax.dot_general(query, fresh(k, 0), LAST, preferred_element_type=F32),
            )
        )
    weights = []
    for k in range(SLOTS):
        score = jnp.where(position < length_ref[k], scores[k][0] * scale, -jnp.inf)
        fresh_score = jnp.where(causal, scores[k][1] * scale, -jnp.inf)
        highest = fresh_score
        for c in range(0, extent, head):
            highest = jnp.maximum(highest, score[:, c : c + head])
        highest = jnp.max(highest, -1, keepdims=True)
        probs, fresh_probs = jnp.exp(score - highest), jnp.exp(fresh_score - highest)
        total = fresh_probs
        for c in range(0, extent, head):
            total = total + probs[:, c : c + head]
        total = jnp.sum(total, -1, keepdims=True)
        weights.append((probs.astype(BF16), fresh_probs.astype(BF16), total))
    for k in range(SLOTS):
        probs, fresh_probs, total = weights[k]
        value = jnp.dot(probs, cache_ref[picked_ref[k], 1], preferred_element_type=F32)
        value = value + jnp.dot(fresh_probs, fresh(k, 1), preferred_element_type=F32)
        answer[pl.ds(k, many, stride=SLOTS), :] = value / total
    for h in range(heads):
        part = answer[rows * h : rows * (h + 1), :].astype(BF16)
        for m in range(out_ref.shape[0]):
            out_ref[m, :, head * h : head * (h + 1)] = part


def output_kernel(key_ref, att_ref, w_ref, out_ref):
    rows = att_ref.shape[0]
    pick = (lax.broadcasted_iota(I32, (rows, out_ref.shape[0]), 0) == key_ref[...]).astype(BF16)
    att = lax.dot_general(pick, att_ref[...], FIRST, preferred_element_type=F32).astype(BF16)
    core = lax.axis_index("sample") % 2
    block = w_ref.shape[0] // 2
    for c in range(0, 2 * block, 256):
        out = lax.dot_general(
            att, w_ref[c : c + 256, :], LAST, preferred_element_type=F32
        ).astype(BF16)
        at = core * block if c < block else (1 - core) * block
        columns = pl.ds(pl.multiple_of(at + c % block, 256), 256)
        out_ref[:, columns] = out


def call(kernel, name, out_shape, specs, scratch=(), vmem=24, cost=None):
    return pl.pallas_call(
        kernel,
        out_shape=out_shape,
        in_specs=specs,
        out_specs=jax.tree.map(lambda _: VMEM, out_shape),
        scratch_shapes=list(scratch),
        name=name,
        cost_estimate=cost,
        compiler_params=pltpu.CompilerParams(vmem_limit_bytes=vmem << 20),
    )


def per_device(x, gain, probe, paired, final, memory, ids, extents):
    steps, held, width = x.shape
    survivors = ids.shape[0]
    owned, _, _, extent, head = memory.shape
    block, _, q_width = probe.shape
    heads = q_width // head
    kv_width = paired.shape[2]
    chips = lax.axis_size("sample") // 2
    chip_block = 2 * block
    rows = steps * survivors
    slot_rows = steps * SLOTS
    shape = jax.ShapeDtypeStruct

    probe, paired, final = (w.reshape(block, w.shape[2]) for w in (probe, paired, final))

    normed = call(
        normalize_kernel,
        "normalize",
        shape((chips, steps * held, chip_block), BF16),
        [ANY, ANY],
        [
            pltpu.VMEM((steps, held, width), BF16),
            pltpu.VMEM((width,), BF16),
            pltpu.VMEM((steps * held, width), F32),
            pltpu.SemaphoreType.DMA((2,)),
        ],
        vmem=60,
    )(x, gain)
    normed, final_out = lax.optimization_barrier((normed, final))
    probe2, paired2, final2 = (send(w, to_core) for w in (probe, paired, final_out))
    near = exchange_rows(normed)

    s = lax.axis_index("sample")
    core, x_at = s & 1, (s >> 1) & 3
    bits = owned.bit_length() - 1
    ids, probe2, paired2 = lax.optimization_barrier((ids, probe2, paired2))
    code = lax.optimization_barrier(ids ^ (s << bits))
    owner = (code >> bits) ^ s
    at = jnp.arange(survivors, dtype=I32)
    slot = jnp.sum(
        ((owner[:, None] == owner[None, :]) & (at[None, :] < at[:, None])).astype(I32), 1
    )
    key, key_back = (
        jnp.where(
            (owner & 1) == core,
            entry(np.argsort(order), owner >> 1) * slot_rows + slot,
            -(1 << 20),
        )
        for order in (QUERY_ORDER, ATTENDED_ORDER)
    )
    q = jnp.arange(rows, dtype=I32)
    n, held_at, step_at = q // (steps * held), q % held, q // held % steps * SLOTS
    this_core = core ^ (n // 8)
    source = (2 * entry(ROWS_ORDER, n % 8) + this_core) * held + held_at
    target_t = entry(OUT_ORDER, n % 8)
    target = (target_t // 4 * 8 + summed_at(x_at, target_t % 4) * 2 + this_core) * held + held_at
    key_in, key_out = (
        (jnp.sum(jnp.where(at[:, None] == j[None, :], keys[:, None], 0), 0) + step_at).reshape(1, rows)
        for j, keys in ((source, key), (target, key_back))
    )
    mine = (owner[:, None] == s) & (slot[:, None] == jnp.arange(SLOTS, dtype=I32)[None, :])
    picked = jnp.sum(jnp.where(mine, (code & (owned - 1))[:, None], 0), 0)
    row_at = s * owned + picked
    length = jnp.sum(
        jnp.where(row_at[:, None] == jnp.arange(extents.shape[0], dtype=I32)[None, :], extents[None, :], 0), 1
    )
    weights = jnp.concatenate([probe, probe2], 0)
    kv_weights = jnp.concatenate([paired, paired2], 0)
    near, key_in, key_out, picked, length, weights, kv_weights = lax.optimization_barrier(
        (near, key_in, key_out, picked, length, weights, kv_weights)
    )
    near = near.reshape(rows // 2, chip_block)
    far = send(near, to_core)

    partial = call(
        project_kernel,
        "project",
        shape((chips, slot_rows, q_width + kv_width), BF16),
        [VMEM] * 5,
        [pltpu.VMEM((rows, chip_block), BF16)],
    )(key_in, near, far, weights, kv_weights)
    attended = call(
        functools.partial(attend_kernel, heads, steps),
        "attend",
        shape((chips, slot_rows, q_width), BF16),
        [SMEM, SMEM, VMEM, VMEM],
        [
            pltpu.VMEM((slot_rows * (heads + 2), head), F32),
            pltpu.VMEM((slot_rows * heads, head), F32),
        ],
        vmem=48,
    )(picked, length, exchange_chips(partial, QUERY_ORDER), memory.reshape(owned, 2, extent, head))
    attended = exchange_chips(attended, ATTENDED_ORDER).reshape(rows, q_width)
    attended, final = lax.optimization_barrier((attended, jnp.concatenate([final, final2], 0)))
    sent, kept = (
        call(
            output_kernel,
            "output",
            shape((rows // 2, chip_block), BF16),
            [VMEM] * 3,
            cost=pl.CostEstimate(
                flops=rows * chip_block * q_width, bytes_accessed=4 << 20, transcendentals=0
            ),
        )(key_out[:, at : at + rows // 2], attended, final)
        for at in (rows // 2, 0)
    )
    out = kept + send(sent, to_core)
    out = exchange_heads(out.reshape(8, steps * held, chip_block))
    out = jnp.sum(out.astype(F32), 0).astype(BF16).reshape(steps, held, chip_block)
    return send(out, to_rows)


def solution(mesh):
    placed = (
        P(None, "sample", None),
        P(),
        P("sample", "tensor", None),
        P("sample", "tensor", None),
        P("sample", "tensor", None),
        P("sample", "tensor", None, None, None),
        P(),
        P(),
    )
    return jax.shard_map(
        per_device,
        mesh=mesh,
        in_specs=placed,
        out_specs=P(None, "sample", "tensor"),
        check_vma=False,
    )
```
